32 devices in a mesh: grp: 2 (over x), lon: 16 (over z, y, core).
Axes of the slice: x: 2, y: 2, z: 4, core: 2. Of those that a mesh axis runs over, the one named last changes fastest.
Arguments:
- state: bfloat16 [256, 256, 300], P(None, ('grp', 'lon')), parts along dimension 1, may hold values from -6 to 6
- ocean_mask: int32 [256, 128], P(None, 'lon'), may hold values from 0 to 1, as said below
- fold_map: int32 [128], replicated, may hold values from 0 to 127, as said below
- w_first: bfloat16 [3, 3, 300, 256], replicated, may hold values from -0.125 to 0.125
- b_first: float32 [256], replicated, may hold values from -3 to 3
- w_second: bfloat16 [3, 3, 256, 256], replicated, may hold values from -0.125 to 0.125
- b_second: float32 [256], replicated, may hold values from -3 to 3
Outputs:
- features: bfloat16 [256, 256, 256], P(None, ('grp', 'lon')), parts along dimension 1
The draws below stay inside these ranges and needn't reach their ends.
There are 2 independent parts, one for each index of `grp`. The reference program is written for one: setup_inputs(seed, part) draws one part's arguments, and reference() takes and returns one part's arrays. A program takes and returns all parts, laid end to end along the dimension named above; an argument that names none is the same for every part. Nothing has to cross between parts.
Inputs may be any that keep to these rules, and one draw needn't show every extreme that they name: `ocean_mask`: 1 marks ocean, 0 land; the ocean share varies from column to column. A reflection: (fold_map[i] + i) mod 128 is the same for every i.
All inputs are finite; a program needn't handle non-finite values.
Results may differ from the reference program's by a relative error of at most 0.004.
Values may be sent and summed in bfloat16 or wider, within the bound.
A program may use at most 64 MiB of HBM per device.

```python
import jax
import jax.numpy as jnp

C_IN = 300
HID = 256
LAT = 256
NLON = 128


def draw_ocean_mask(key, part):
    key_col, key_cell = jax.random.split(key)
    share = jax.random.randint(key_col, (NLON,), 25, 101)
    cells = jax.random.randint(key_cell, (LAT, NLON), 0, 100)
    return (cells < share[None, :]).astype(jnp.int32)


def draw_fold_map(key, part):
    pivot = jax.random.randint(key, (), 0, NLON)
    return ((pivot - jnp.arange(NLON, dtype=jnp.int32)) % NLON).astype(jnp.int32)


def block_levels(stream_key, extent, cuts, low, high):
    loudness = 1.0
    for dim, shards_of in cuts:
        draws = jax.random.uniform(jax.random.fold_in(jax.random.fold_in(stream_key, 6), dim), (shards_of,), jnp.float32, low / len(cuts), high / len(cuts))
        loudness = loudness * jnp.repeat(jnp.exp(draws), extent[dim] // shards_of).reshape((-1,) + (1,) * (len(extent) - 1 - dim))
    return loudness


def scatter_about(own_key, shape, width, bound, cuts=(), held_as=jnp.bfloat16):
    result = width * jax.random.normal(own_key, shape, jnp.float32)
    if cuts:
        result = result * block_levels(own_key, shape, cuts, -0.22, 0.18)
    return jnp.clip(result, -bound, bound).astype(held_as)


def setup_inputs(seed: int = 0, part: int = 0) -> dict:
    seeds = jax.random.split(jax.random.key(seed), 8)
    part_splits = jax.random.split(jax.random.fold_in(seeds[7], part), 8)
    state = scatter_about(part_splits[0], (LAT, NLON, C_IN), 1.0, 6.0, ((1, 16),))
    ocean_mask = draw_ocean_mask(jax.random.fold_in(seeds[7], 71), part)
    fold_map = draw_fold_map(jax.random.fold_in(seeds[7], 71), part)
    w_first = scatter_about(seeds[3], (3, 3, C_IN, HID), (9 * C_IN) ** -0.5, 0.125)
    b_first = scatter_about(seeds[4], (HID,), 0.5, 3.0, (), jnp.float32)
    w_second = scatter_about(seeds[5], (3, 3, HID, HID), (9 * HID) ** -0.5, 0.125)
    b_second = scatter_about(seeds[6], (HID,), 0.5, 3.0, (), jnp.float32)
    return {"state": state, "ocean_mask": ocean_mask, "fold_map": fold_map, "w_first": w_first, "b_first": b_first, "w_second": w_second, "b_second": b_second}


def gelu(value):
    return 0.5 * value * (1.0 + jnp.tanh(0.7978845608 * (value + 0.044715 * value * value * value)))


def conv_taps(padded, weight, rows, cols):
    chans = padded.shape[-1]
    total = jnp.zeros((rows * cols, weight.shape[-1]), jnp.float32)
    for shift_y in range(3):
        for shift_x in range(3):
            tap = padded[shift_y:shift_y + rows, shift_x:shift_x + cols].reshape(rows * cols, chans)
            total = total + jnp.dot(tap, weight[shift_y, shift_x], preferred_element_type=jnp.float32)
    return total.reshape(rows, cols, weight.shape[-1])


def extend(field, ghost):
    zeros = jnp.zeros((1,) + field.shape[1:], field.dtype)
    tall = jnp.concatenate([zeros, field, ghost[None]], axis=0)
    return jnp.concatenate([tall[:, -1:], tall, tall[:, :1]], axis=1)


def reference(state, ocean_mask, fold_map, w_first, b_first, w_second, b_second):
    rows, cols, chans = state.shape
    masked = state * ocean_mask.astype(jnp.bfloat16)[:, :, None]
    signs = jnp.where(jnp.arange(chans) < chans // 2, -1.0, 1.0).astype(jnp.bfloat16)
    ghost = jnp.take(masked[rows - 1], fold_map.astype(jnp.int32), axis=0) * signs
    first = conv_taps(extend(masked, ghost), w_first, rows, cols)
    mask_f = ocean_mask.astype(jnp.float32)[:, :, None]
    hidden = (gelu(first + b_first) * mask_f).astype(jnp.bfloat16)
    ghost_hidden = jnp.take(hidden[rows - 1], fold_map.astype(jnp.int32), axis=0)
    second = conv_taps(extend(hidden, ghost_hidden), w_second, rows, cols)
    return ((second + b_second) * mask_f).astype(jnp.bfloat16)
```

```python
import functools

import jax
import jax.numpy as jnp
from jax import lax
from jax.experimental import pallas as pl
from jax.experimental.pallas import tpu as pltpu
from jax.sharding import PartitionSpec as P

LANES = 128
TAIL_SLOT = 64
MESH = pl.DeviceIdType.MESH
F32 = jnp.float32
BF16 = jnp.bfloat16


def gelu(value):
    return 0.5 * value * (1.0 + jnp.tanh(0.7978845608 * (value + 0.044715 * value * value * value)))


def kernel(
    x_hbm, m_ref, fold_ref, w1_hbm, b1_ref, w2_hbm, b2_ref, out_ref,
    xv, xs, w1, w2, wt, cols1, tails, cols2, top1, top2, mcol,
    load_sem, t1_send, t1_recv, t2_send, t2_recv, x_send, x_recv, h_send, h_recv,
):
    n = lax.axis_size("lon")
    me = lax.axis_index("lon")
    right, left = lax.rem(me + 1, n), lax.rem(me + n - 1, n)
    chans, width, rows = x_hbm.shape
    main = w1.shape[-1]
    hid = w2.shape[-1]
    padded = main + LANES
    total = n * width

    barrier = pltpu.get_barrier_semaphore()

    def greet(i, _):
        pl.semaphore_signal(
            barrier, inc=1, device_id={"lon": lax.rem(me + i, n)}, device_id_type=MESH
        )
        return 0

    lax.fori_loop(1, n, greet, 0)
    load_x = pltpu.make_async_copy(x_hbm, xv, load_sem.at[0])
    load_1 = pltpu.make_async_copy(w1_hbm, w1, load_sem.at[1])
    load_2 = pltpu.make_async_copy(w2_hbm, w2, load_sem.at[2])
    load_x.start()
    load_1.start()
    load_2.start()

    wt[...] = jnp.zeros_like(wt)
    halves = rows // LANES
    for h in range(halves):
        xs[h, chans * width :, :] = jnp.zeros((xs.shape[1] - chans * width, LANES), F32)
    mask = m_ref[...].astype(F32)
    mask_t = jnp.transpose(jnp.concatenate([mask] * (LANES // width), axis=0))
    for c in range(width):
        mcol[c] = mask_t[:, c : c + 1]
    row = lax.broadcasted_iota(jnp.int32, (rows, 1), 0)
    first_row, last_row = row == 0, row == rows - 1
    last_tile = lax.broadcasted_iota(jnp.int32, (16, 1), 0) == 15

    def build1(slot, value):
        up = jnp.where(first_row, 0.0, pltpu.roll(value, 1, 0))
        down = jnp.where(last_row, 0.0, pltpu.roll(value, rows - 1, 0))
        cols1[slot, :, 0:main] = up[:, :main].astype(BF16)
        cols1[slot, :, 2 * main : 3 * main] = down[:, :main].astype(BF16)
        pair = up[:, main:] + pltpu.roll(value[:, main:], TAIL_SLOT, 1)
        cols1[slot, :, 3 * main : 3 * main + LANES] = pair.astype(BF16)
        cols1[slot, :, 3 * main + LANES :] = down[:, main:].astype(BF16)

    def build2(slot, value):
        up = jnp.where(first_row, 0.0, pltpu.roll(value, 1, 0))
        down = jnp.where(last_row, 0.0, pltpu.roll(value, rows - 1, 0))
        cols2[slot, :, 0:hid] = up.astype(BF16)
        cols2[slot, :, 2 * hid : 3 * hid] = down.astype(BF16)

    def patch(buffer, slot, lo, hi, ghost):
        old = buffer[slot, rows - 16 :, lo:hi].astype(F32)
        buffer[slot, rows - 16 :, lo:hi] = jnp.where(last_tile, ghost, old).astype(BF16)

    def folded(top, slot):
        column = lax.rem(me * width + slot - 1 + total, total)
        return top[pl.ds(fold_ref[column], 1), :]

    signs = jnp.where(
        lax.broadcasted_iota(jnp.int32, (1, padded), 1) < chans // 2, -1.0, 1.0
    )

    def fold1(slot, _):
        ghost = folded(top1, slot) * signs
        patch(cols1, slot, 2 * main, 3 * main, ghost[:, :main])
        patch(cols1, slot, 3 * main + LANES, 3 * main + 2 * LANES, ghost[:, main:])
        return 0

    def fold2(slot, _):
        patch(cols2, slot, 2 * hid, 3 * hid, folded(top2, slot))
        return 0

    def top_copy(top, send, recv, i):
        peer = lax.rem(me + i, n)
        block = pl.ds(pl.multiple_of(me * width, width), width)
        return pltpu.make_async_remote_copy(
            src_ref=top.at[block], dst_ref=top.at[block], send_sem=send.at[i],
            recv_sem=recv.at[i], device_id={"lon": peer}, device_id_type=MESH,
        )

    def send_tops(top, send, recv):
        def one(i, _):
            top_copy(top, send, recv, i).start()
            return 0

        lax.fori_loop(1, n, one, 0)

    def wait_tops(top, send, recv):
        def one(i, _):
            top_copy(top, send, recv, i).wait()
            return 0

        lax.fori_loop(1, n, one, 0)

    def halo(src, dst, send, recv, k, peer):
        return pltpu.make_async_remote_copy(
            src_ref=src, dst_ref=dst, send_sem=send.at[k], recv_sem=recv.at[k],
            device_id={"lon": peer}, device_id_type=MESH,
        )

    load_x.wait()
    masked = (xv[...].astype(F32) * mask[None]).reshape(chans * width, rows)
    for h in range(halves):
        xs[h, 0 : chans * width, :] = masked[:, h * LANES : (h + 1) * LANES]

    def spread(c, _):
        value = jnp.concatenate(
            [jnp.transpose(xs[h, pl.ds(c, padded, stride=width), :]) for h in range(halves)], axis=0
        )
        cols1[c + 1, :, main : 2 * main] = value[:, :main].astype(BF16)
        tails[c + 1] = value[:, main:].astype(BF16)
        top1[pl.ds(me * width + c, 1), :] = value[rows - 1 :, :]
        build1(c + 1, value)
        return 0

    lax.fori_loop(0, width, spread, 0)
    pl.semaphore_wait(barrier, n - 1)
    send_tops(top1, t1_send, t1_recv)
    mid1, mid2 = pl.ds(main, main), pl.ds(hid, hid)
    x_halos = [
        halo(cols1.at[1, :, mid1], cols1.at[width + 1, :, mid1], x_send, x_recv, 0, left),
        halo(tails.at[1], tails.at[width + 1], x_send, x_recv, 1, left),
        halo(cols1.at[width, :, mid1], cols1.at[0, :, mid1], x_send, x_recv, 2, right),
        halo(tails.at[width], tails.at[0], x_send, x_recv, 3, right),
    ]
    for copy in x_halos:
        copy.start()

    load_1.wait()
    for dx in range(3):
        for dy in range(3):
            wt[dx, TAIL_SLOT * dy : TAIL_SLOT * dy + chans - main, :] = w1[dy, dx, main:chans, :]

    wait_tops(top1, t1_send, t1_recv)
    lax.fori_loop(1, width + 1, fold1, 0)

    def first(ca, cb):
        acc = None
        for dx in range(3):
            lhs = jnp.concatenate([cols1[ca + dx], cols1[cb + dx]], axis=0)
            rhs = jnp.concatenate([w1[dy, dx, :main, :] for dy in range(3)] + [wt[dx]], axis=0)
            part = jnp.dot(lhs, rhs, preferred_element_type=F32)
            acc = part if acc is None else acc + part
        for k, c in enumerate((ca, cb)):
            value = gelu(acc[k * rows : (k + 1) * rows] + b1_ref[...]) * mcol[c]
            value = value.astype(BF16)
            cols2[c + 1, :, hid : 2 * hid] = value
            value = value.astype(F32)
            top2[pl.ds(me * width + c, 1), :] = value[rows - 1 :, :]
            build2(c + 1, value)

    def second(ca, cb):
        acc = None
        for dx in range(3):
            lhs = jnp.concatenate([cols2[ca + dx], cols2[cb + dx]], axis=0)
            rhs = jnp.concatenate([w2[dy, dx] for dy in range(3)], axis=0)
            part = jnp.dot(lhs, rhs, preferred_element_type=F32)
            acc = part if acc is None else acc + part
        for k, c in enumerate((ca, cb)):
            value = (acc[k * rows : (k + 1) * rows] + b2_ref[...]) * mcol[c]
            out_ref[c] = value.astype(BF16)

    def inner(step):
        def one(i, _):
            step(2 * i + 1, 2 * i + 2)
            return 0

        lax.fori_loop(0, (width - 2) // 2, one, 0)

    inner(first)
    for copy in x_halos:
        copy.wait()
    for slot in (0, width + 1):
        mid = jnp.concatenate([cols1[slot, :, main : 2 * main], tails[slot]], axis=1)
        build1(slot, mid.astype(F32))
        fold1(slot, 0)
    first(0, width - 1)

    send_tops(top2, t2_send, t2_recv)
    h_halos = [
        halo(cols2.at[1, :, mid2], cols2.at[width + 1, :, mid2], h_send, h_recv, 0, left),
        halo(cols2.at[width, :, mid2], cols2.at[0, :, mid2], h_send, h_recv, 1, right),
    ]
    for copy in h_halos:
        copy.start()
    load_2.wait()
    wait_tops(top2, t2_send, t2_recv)
    lax.fori_loop(1, width + 1, fold2, 0)
    inner(second)
    for copy in h_halos:
        copy.wait()
    for slot in (0, width + 1):
        build2(slot, cols2[slot, :, hid : 2 * hid].astype(F32))
        fold2(slot, 0)
    second(0, width - 1)


def local(n, state, ocean_mask, fold_map, w_first, b_first, w_second, b_second):
    rows, width, chans = state.shape
    hid = w_first.shape[-1]
    out = w_second.shape[-1]
    main = chans // LANES * LANES
    vmem = pl.BlockSpec(memory_space=pltpu.VMEM)
    hbm = pl.BlockSpec(memory_space=pl.ANY)
    result = pl.pallas_call(
        kernel,
        out_shape=jax.ShapeDtypeStruct((width, rows, out), BF16),
        in_specs=[hbm, vmem, pl.BlockSpec(memory_space=pltpu.SMEM), hbm, vmem, hbm, vmem],
        out_specs=vmem,
        scratch_shapes=[
            pltpu.VMEM((chans, width, rows), BF16),
            pltpu.VMEM((rows // LANES, (main + LANES) * width, LANES), F32),
            pltpu.VMEM(w_first.shape, BF16),
            pltpu.VMEM(w_second.shape, BF16),
            pltpu.VMEM((3, 2 * LANES, hid), BF16),
            pltpu.VMEM((width + 2, rows, 3 * main + 2 * LANES), BF16),
            pltpu.VMEM((width + 2, rows, LANES), BF16),
            pltpu.VMEM((width + 2, rows, 3 * hid), BF16),
            pltpu.VMEM((n * width, main + LANES), F32),
            pltpu.VMEM((n * width, hid), F32),
            pltpu.VMEM((width, rows, 1), F32),
            pltpu.SemaphoreType.DMA((3,)),
            pltpu.SemaphoreType.DMA((n,)),
            pltpu.SemaphoreType.DMA((n,)),
            pltpu.SemaphoreType.DMA((n,)),
            pltpu.SemaphoreType.DMA((n,)),
            pltpu.SemaphoreType.DMA((4,)),
            pltpu.SemaphoreType.DMA((4,)),
            pltpu.SemaphoreType.DMA((2,)),
            pltpu.SemaphoreType.DMA((2,)),
        ],
        compiler_params=pltpu.CompilerParams(
            collective_id=0, has_side_effects=True, vmem_limit_bytes=56 * 1024 * 1024
        ),
        name="masked_conv_pair",
    )(
        jnp.transpose(state, (2, 1, 0)),
        jnp.transpose(ocean_mask),
        fold_map,
        w_first,
        b_first.reshape(1, hid),
        w_second,
        b_second.reshape(1, out),
    )
    return jnp.transpose(result, (1, 0, 2))


def solution(mesh):
    return jax.shard_map(
        functools.partial(local, mesh.shape["lon"]),
        mesh=mesh,
        in_specs=(P(None, ("grp", "lon"), None), P(None, "lon"), P(), P(), P(), P(), P()),
        out_specs=P(None, ("grp", "lon"), None),
        check_vma=False,
    )
```

```python
import functools

import jax
import jax.numpy as jnp
from jax import lax
from jax.experimental import pallas as pl
from jax.experimental.pallas import tpu as pltpu
from jax.sharding import PartitionSpec as P

LANES = 128
TAIL_SLOT = 64
MESH = pl.DeviceIdType.MESH
F32 = jnp.float32
BF16 = jnp.bfloat16


def gelu(value):
    return 0.5 * value * (1.0 + jnp.tanh(0.7978845608 * (value + 0.044715 * value * value * value)))


def kernel(
    x_hbm, m_ref, fold_ref, w1_hbm, b1_ref, w2_hbm, b2_ref, out_ref,
    xv, xs, w1, w2, wt, cols1, tails, cols2, top1, top2, own1, all1, all2, part, pre, mcol,
    load_sem, t1_send, t1_recv, t2_send, t2_recv, x_send, x_recv, h_send, h_recv,
):
    n = lax.axis_size("lon")
    me = lax.axis_index("lon")
    right, left = lax.rem(me + 1, n), lax.rem(me + n - 1, n)
    chans, width, rows = x_hbm.shape
    main = w1.shape[-1]
    hid = w2.shape[-1]
    padded = main + LANES
    total = n * width

    barrier = pltpu.get_barrier_semaphore()

    def greet(i, _):
        pl.semaphore_signal(
            barrier, inc=1, device_id={"lon": lax.rem(me + i, n)}, device_id_type=MESH
        )
        return 0

    lax.fori_loop(1, n, greet, 0)
    load_x = pltpu.make_async_copy(x_hbm, xv, load_sem.at[0])
    load_1 = pltpu.make_async_copy(w1_hbm, w1, load_sem.at[1])
    load_2 = pltpu.make_async_copy(w2_hbm, w2, load_sem.at[2])
    load_x.start()
    load_1.start()
    load_2.start()

    wt[...] = jnp.zeros_like(wt)
    halves = rows // LANES
    for h in range(halves):
        xs[h, chans * width :, :] = jnp.zeros((xs.shape[1] - chans * width, LANES), F32)
    mask = m_ref[...].astype(F32)
    mask_t = jnp.transpose(jnp.concatenate([mask] * (LANES // width), axis=0))
    for c in range(width):
        mcol[c] = mask_t[:, c : c + 1]
    row = lax.broadcasted_iota(jnp.int32, (rows, 1), 0)
    first_row, last_row = row == 0, row == rows - 1
    last_tile = lax.broadcasted_iota(jnp.int32, (16, 1), 0) == 15

    def build1(slot, value):
        up = jnp.where(first_row, 0.0, pltpu.roll(value, 1, 0))
        down = jnp.where(last_row, 0.0, pltpu.roll(value, rows - 1, 0))
        cols1[slot, :, 0:main] = up[:, :main].astype(BF16)
        cols1[slot, :, 2 * main : 3 * main] = down[:, :main].astype(BF16)
        pair = up[:, main:] + pltpu.roll(value[:, main:], TAIL_SLOT, 1)
        cols1[slot, :, 3 * main : 3 * main + LANES] = pair.astype(BF16)
        cols1[slot, :, 3 * main + LANES :] = down[:, main:].astype(BF16)

    def build2(slot, value):
        up = jnp.where(first_row, 0.0, pltpu.roll(value, 1, 0))
        down = jnp.where(last_row, 0.0, pltpu.roll(value, rows - 1, 0))
        cols2[slot, :, 0:hid] = up.astype(BF16)
        cols2[slot, :, 2 * hid : 3 * hid] = down.astype(BF16)

    def folded(top, slot):
        column = lax.rem(me * width + slot - 1 + total, total)
        return top[pl.ds(fold_ref[column], 1), :]

    signs = jnp.where(
        lax.broadcasted_iota(jnp.int32, (1, padded), 1) < chans // 2, -1.0, 1.0
    )

    def ghosts(top):
        lines = [folded(top, slot) for slot in range(width + 2)]
        lines = lines + [jnp.zeros_like(lines[0])] * (2 * width - len(lines))
        stack = jnp.concatenate(lines, axis=0)
        return [stack[dx : dx + width] for dx in range(3)]

    def twice(block):
        return jnp.concatenate([block, block], axis=0).astype(BF16)

    def top_copy(top, send, recv, i):
        peer = lax.rem(me + i, n)
        return pltpu.make_async_remote_copy(
            src_ref=top.at[me], dst_ref=top.at[me], send_sem=send.at[i],
            recv_sem=recv.at[i], device_id={"lon": peer}, device_id_type=MESH,
        )

    def send_tops(top, send, recv):
        def one(i, _):
            top_copy(top, send, recv, i).start()
            return 0

        lax.fori_loop(1, n, one, 0)

    def wait_tops(top, send, recv):
        def one(i, _):
            top_copy(top, send, recv, i).wait()
            return 0

        lax.fori_loop(1, n, one, 0)

    def halo(src, dst, send, recv, k, peer):
        return pltpu.make_async_remote_copy(
            src_ref=src, dst_ref=dst, send_sem=send.at[k], recv_sem=recv.at[k],
            device_id={"lon": peer}, device_id_type=MESH,
        )

    load_x.wait()
    masked = (xv[...].astype(F32) * mask[None]).reshape(chans * width, rows)
    for h in range(halves):
        xs[h, 0 : chans * width, :] = masked[:, h * LANES : (h + 1) * LANES]

    def spread(c, _):
        value = jnp.concatenate(
            [jnp.transpose(xs[h, pl.ds(c, padded, stride=width), :]) for h in range(halves)], axis=0
        )
        cols1[c + 1, :, main : 2 * main] = value[:, :main].astype(BF16)
        tails[c + 1] = value[:, main:].astype(BF16)
        own1[pl.ds(c, 1), :] = value[rows - 1 :, :]
        build1(c + 1, value)
        return 0

    lax.fori_loop(0, width, spread, 0)
    top1[me] = own1[...].astype(BF16)
    mid1, mid2 = pl.ds(main, main), pl.ds(hid, hid)
    x_halos = [
        halo(cols1.at[1, :, mid1], cols1.at[width + 1, :, mid1], x_send, x_recv, 0, left),
        halo(tails.at[1], tails.at[width + 1], x_send, x_recv, 1, left),
        halo(cols1.at[width, :, mid1], cols1.at[0, :, mid1], x_send, x_recv, 2, right),
        halo(tails.at[width], tails.at[0], x_send, x_recv, 3, right),
    ]
    load_1.wait()
    for dx in range(3):
        for dy in range(3):
            wt[dx, TAIL_SLOT * dy : TAIL_SLOT * dy + chans - main, :] = w1[dy, dx, main:chans, :]

    tile = rows - 16

    def weight1(dx):
        return jnp.concatenate([w1[dy, dx, :main, :] for dy in range(3)] + [wt[dx]], axis=0)

    def weight2(dx):
        return jnp.concatenate([w2[dy, dx] for dy in range(3)], axis=0)

    def dot(lhs, rhs):
        return jnp.dot(lhs, rhs, preferred_element_type=F32)

    def pair_of(buffer, weight, ca, cb):
        acc = None
        for dx in range(3):
            lhs = jnp.concatenate([buffer[ca + dx], buffer[cb + dx]], axis=0)
            term = dot(lhs, weight(dx))
            acc = term if acc is None else acc + term
        return acc

    def edges_of(buffer, weight):
        both = jnp.concatenate([buffer[1], buffer[width]], axis=0)
        acc = dot(both, weight(1))
        part[0] = acc[:rows] + dot(buffer[2], weight(2))
        part[1] = acc[rows:] + dot(buffer[width - 1], weight(0))

    def activate(c, value):
        value = (gelu(value) * mcol[c]).astype(BF16)
        cols2[c + 1, :, hid : 2 * hid] = value
        value = value.astype(F32)
        build2(c + 1, value)

    def first(ca, cb):
        acc = pair_of(cols1, weight1, ca, cb) + b1_ref[...]
        pre[pl.ds(ca, 1), :] = acc[rows - 1 : rows, :]
        pre[pl.ds(cb, 1), :] = acc[2 * rows - 1 :, :]
        activate(ca, acc[:rows])
        activate(cb, acc[rows:])

    def edge(buffer, weight, side):
        slot, dx = ((0, 0), (width + 1, 2))[side]
        return part[side] + dot(buffer[slot], weight(dx))

    mask_top = mask[:, rows - 1 :]

    def first_edge(side):
        c = side * (width - 1)
        acc = edge(cols1, weight1, side) + b1_ref[...]
        pre[c : c + 1, :] = acc[rows - 1 :, :]
        activate(c, acc)

    def first_top():
        fold = [g * signs for g in ghosts(all1)]
        extra = pre[...]
        for dx in range(3):
            extra = extra + dot(twice(fold[dx][:, :main]), w1[2, dx, :main, :])[:width]
            extra = extra + dot(twice(fold[dx][:, main:]), wt[dx, LANES:, :])[:width]
        hidden = (gelu(extra) * mask_top).astype(BF16).astype(F32)
        top2[me] = hidden.astype(BF16)
        for c in range(width):
            old = cols2[c + 1, tile:, hid : 2 * hid].astype(F32)
            value = jnp.where(last_tile, hidden[c : c + 1], old)
            cols2[c + 1, tile:, hid : 2 * hid] = value.astype(BF16)
            down = jnp.where(last_tile, 0.0, pltpu.roll(value, 15, 0))
            cols2[c + 1, tile:, 2 * hid : 3 * hid] = down.astype(BF16)

    def put(c, value):
        for h in range(hid // LANES):
            part = value[:, h * LANES : (h + 1) * LANES]
            xs[h, pl.ds(c, rows, stride=width), :] = part

    def second(ca, cb):
        acc = pair_of(cols2, weight2, ca, cb) + b2_ref[...]
        put(ca, acc[:rows] * mcol[ca])
        put(cb, acc[rows:] * mcol[cb])

    def second_edge(side):
        c = side * (width - 1)
        put(c, (edge(cols2, weight2, side) + b2_ref[...]) * mcol[c])

    def second_top():
        fold = ghosts(all2)
        extra = None
        for dx in range(3):
            term = dot(twice(fold[dx]), w2[2, dx])[:width]
            extra = term if extra is None else extra + term
        extra = extra * mask_top
        for h in range(hid // LANES):
            at = (rows - 1) * width
            xs[h, at : at + width, :] += extra[:, h * LANES : (h + 1) * LANES]

    def inner(step, lo, hi):
        def one(i, _):
            step(2 * i + 1, 2 * i + 2)
            return 0

        lax.fori_loop(lo, hi, one, 0)

    pairs = (width - 2) // 2
    pl.semaphore_wait(barrier, n - 1)
    send_tops(top1, t1_send, t1_recv)
    for copy in x_halos:
        copy.start()
    edges_of(cols1, weight1)
    inner(first, 0, pairs)
    wait_tops(top1, t1_send, t1_recv)
    all1[...] = top1[...].astype(F32).reshape(all1.shape)
    for copy in x_halos:
        copy.wait()
    for side, slot in enumerate((0, width + 1)):
        mid = jnp.concatenate([cols1[slot, :, main : 2 * main], tails[slot]], axis=1)
        build1(slot, mid.astype(F32))
        first_edge(side)
    first_top()

    h_halos = [
        halo(cols2.at[1, :, mid2], cols2.at[width + 1, :, mid2], h_send, h_recv, 0, left),
        halo(cols2.at[width, :, mid2], cols2.at[0, :, mid2], h_send, h_recv, 1, right),
    ]
    send_tops(top2, t2_send, t2_recv)
    for copy in h_halos:
        copy.start()
    load_2.wait()
    edges_of(cols2, weight2)
    inner(second, 0, pairs)
    wait_tops(top2, t2_send, t2_recv)
    all2[...] = top2[...].astype(F32).reshape(all2.shape)
    for copy in h_halos:
        copy.wait()
    for side, slot in enumerate((0, width + 1)):
        build2(slot, cols2[slot, :, hid : 2 * hid].astype(F32))
        second_edge(side)
    second_top()
    for h in range(hid // LANES):
        block = xs[h, 0 : rows * width, :].reshape(rows, width, LANES)
        out_ref[:, :, h * LANES : (h + 1) * LANES] = block.astype(BF16)


def local(n, state, ocean_mask, fold_map, w_first, b_first, w_second, b_second):
    rows, width, chans = state.shape
    hid = w_first.shape[-1]
    out = w_second.shape[-1]
    main = chans // LANES * LANES
    vmem = pl.BlockSpec(memory_space=pltpu.VMEM)
    hbm = pl.BlockSpec(memory_space=pl.ANY)
    result = pl.pallas_call(
        kernel,
        out_shape=jax.ShapeDtypeStruct((rows, width, out), BF16),
        in_specs=[hbm, vmem, pl.BlockSpec(memory_space=pltpu.SMEM), hbm, vmem, hbm, vmem],
        out_specs=vmem,
        scratch_shapes=[
            pltpu.VMEM((chans, width, rows), BF16),
            pltpu.VMEM((rows // LANES, (main + LANES) * width, LANES), F32),
            pltpu.VMEM(w_first.shape, BF16),
            pltpu.VMEM(w_second.shape, BF16),
            pltpu.VMEM((3, 2 * LANES, hid), BF16),
            pltpu.VMEM((width + 2, rows, 3 * main + 2 * LANES), BF16),
            pltpu.VMEM((width + 2, rows, LANES), BF16),
            pltpu.VMEM((width + 2, rows, 3 * hid), BF16),
            pltpu.VMEM((n, width, main + LANES), BF16),
            pltpu.VMEM((n, width, hid), BF16),
            pltpu.VMEM((width, main + LANES), F32),
            pltpu.VMEM((n * width, main + LANES), F32),
            pltpu.VMEM((n * width, hid), F32),
            pltpu.VMEM((2, rows, hid), F32),
            pltpu.VMEM((width, hid), F32),
            pltpu.VMEM((width, rows, 1), F32),
            pltpu.SemaphoreType.DMA((3,)),
            pltpu.SemaphoreType.DMA((n,)),
            pltpu.SemaphoreType.DMA((n,)),
            pltpu.SemaphoreType.DMA((n,)),
            pltpu.SemaphoreType.DMA((n,)),
            pltpu.SemaphoreType.DMA((4,)),
            pltpu.SemaphoreType.DMA((4,)),
            pltpu.SemaphoreType.DMA((2,)),
            pltpu.SemaphoreType.DMA((2,)),
        ],
        compiler_params=pltpu.CompilerParams(
            collective_id=0, has_side_effects=True, vmem_limit_bytes=56 * 1024 * 1024
        ),
        name="masked_conv_pair",
    )(
        jnp.transpose(state, (2, 1, 0)),
        jnp.transpose(ocean_mask),
        fold_map,
        w_first,
        b_first.reshape(1, hid),
        w_second,
        b_second.reshape(1, out),
    )
    return result


def solution(mesh):
    return jax.shard_map(
        functools.partial(local, mesh.shape["lon"]),
        mesh=mesh,
        in_specs=(P(None, ("grp", "lon"), None), P(None, "lon"), P(), P(), P(), P(), P()),
        out_specs=P(None, ("grp", "lon"), None),
        check_vma=False,
    )
```

```python
import functools

import jax
import jax.numpy as jnp
from jax import lax
from jax.experimental import pallas as pl
from jax.experimental.pallas import tpu as pltpu
from jax.sharding import PartitionSpec as P

LANES = 128
TAIL_SLOT = 64
MESH = pl.DeviceIdType.MESH
F32 = jnp.float32
BF16 = jnp.bfloat16


def gelu(value):
    return 0.5 * value * (1.0 + jnp.tanh(0.7978845608 * (value + 0.044715 * value * value * value)))


def kernel(
    x_hbm, m_ref, fold_ref, w1_hbm, b1_ref, w2_hbm, b2_ref, out_ref,
    xv, xs, w1, w2, wt, cols1, tails, cols2, top1, top2, own1, all1, all2, part, pre, mcol,
    load_sem, t1_send, t1_recv, t2_send, t2_recv, x_send, x_recv, h_send, h_recv,
):
    n = lax.axis_size("lon")
    me = lax.axis_index("lon")
    right, left = lax.rem(me + 1, n), lax.rem(me + n - 1, n)
    chans, width, rows = x_hbm.shape
    main = w1.shape[-1]
    hid = w2.shape[-1]
    padded = main + LANES
    total = n * width

    barrier = pltpu.get_barrier_semaphore()

    def greet(i, _):
        pl.semaphore_signal(
            barrier, inc=1, device_id={"lon": lax.rem(me + i, n)}, device_id_type=MESH
        )
        return 0

    lax.fori_loop(1, n, greet, 0)
    load_x = pltpu.make_async_copy(x_hbm, xv, load_sem.at[0])
    load_1 = pltpu.make_async_copy(w1_hbm, w1, load_sem.at[1])
    load_2 = pltpu.make_async_copy(w2_hbm, w2, load_sem.at[2])
    load_x.start()
    load_1.start()
    load_2.start()

    wt[...] = jnp.zeros_like(wt)
    halves = rows // LANES
    for h in range(halves):
        xs[h, chans * width :, :] = jnp.zeros((xs.shape[1] - chans * width, LANES), F32)
    mask = m_ref[...].astype(F32)
    mask_t = jnp.transpose(jnp.concatenate([mask] * (LANES // width), axis=0))
    for c in range(width):
        mcol[c] = mask_t[:, c : c + 1]
    row = lax.broadcasted_iota(jnp.int32, (rows, 1), 0)
    first_row, last_row = row == 0, row == rows - 1
    last_tile = lax.broadcasted_iota(jnp.int32, (16, 1), 0) == 15

    def build1(slot, value):
        up = jnp.where(first_row, 0.0, pltpu.roll(value, 1, 0))
        down = jnp.where(last_row, 0.0, pltpu.roll(value, rows - 1, 0))
        cols1[slot, :, 0:main] = up[:, :main].astype(BF16)
        cols1[slot, :, 2 * main : 3 * main] = down[:, :main].astype(BF16)
        pair = up[:, main:] + pltpu.roll(value[:, main:], TAIL_SLOT, 1)
        cols1[slot, :, 3 * main : 3 * main + LANES] = pair.astype(BF16)
        cols1[slot, :, 3 * main + LANES :] = down[:, main:].astype(BF16)

    def build2(slot, value):
        up = jnp.where(first_row, 0.0, pltpu.roll(value, 1, 0))
        down = jnp.where(last_row, 0.0, pltpu.roll(value, rows - 1, 0))
        cols2[slot, :, 0:hid] = up.astype(BF16)
        cols2[slot, :, 2 * hid : 3 * hid] = down.astype(BF16)

    def folded(top, slot):
        column = lax.rem(me * width + slot - 1 + total, total)
        return top[pl.ds(fold_ref[column], 1), :]

    signs = jnp.where(
        lax.broadcasted_iota(jnp.int32, (1, padded), 1) < chans // 2, -1.0, 1.0
    )

    def ghosts(top):
        lines = [folded(top, slot) for slot in range(width + 2)]
        lines = lines + [jnp.zeros_like(lines[0])] * (2 * width - len(lines))
        stack = jnp.concatenate(lines, axis=0)
        return [stack[dx : dx + width] for dx in range(3)]

    def twice(block):
        return jnp.concatenate([block, block], axis=0).astype(BF16)

    def top_copy(top, send, recv, i):
        peer = lax.rem(me + i, n)
        return pltpu.make_async_remote_copy(
            src_ref=top.at[me], dst_ref=top.at[me], send_sem=send.at[i],
            recv_sem=recv.at[i], device_id={"lon": peer}, device_id_type=MESH,
        )

    def send_tops(top, send, recv):
        def one(i, _):
            top_copy(top, send, recv, i).start()
            return 0

        lax.fori_loop(1, n, one, 0)

    def wait_tops(top, send, recv):
        def one(i, _):
            top_copy(top, send, recv, i).wait()
            return 0

        lax.fori_loop(1, n, one, 0)

    def halo(src, dst, send, recv, k, peer):
        return pltpu.make_async_remote_copy(
            src_ref=src, dst_ref=dst, send_sem=send.at[k], recv_sem=recv.at[k],
            device_id={"lon": peer}, device_id_type=MESH,
        )

    load_x.wait()
    masked = (xv[...].astype(F32) * mask[None]).reshape(chans * width, rows)
    for h in range(halves):
        xs[h, 0 : chans * width, :] = masked[:, h * LANES : (h + 1) * LANES]

    def spread(c, _):
        value = jnp.concatenate(
            [jnp.transpose(xs[h, pl.ds(c, padded, stride=width), :]) for h in range(halves)], axis=0
        )
        cols1[c + 1, :, main : 2 * main] = value[:, :main].astype(BF16)
        tails[c + 1] = value[:, main:].astype(BF16)
        own1[pl.ds(c, 1), :] = value[rows - 1 :, :]
        build1(c + 1, value)
        return 0

    lax.fori_loop(0, width, spread, 0)
    top1[me] = own1[...].astype(BF16)
    mid1, mid2 = pl.ds(main, main), pl.ds(hid, hid)
    x_halos = [
        halo(cols1.at[1, :, mid1], cols1.at[width + 1, :, mid1], x_send, x_recv, 0, left),
        halo(tails.at[1], tails.at[width + 1], x_send, x_recv, 1, left),
        halo(cols1.at[width, :, mid1], cols1.at[0, :, mid1], x_send, x_recv, 2, right),
        halo(tails.at[width], tails.at[0], x_send, x_recv, 3, right),
    ]
    load_1.wait()
    for dx in range(3):
        for dy in range(3):
            wt[dx, TAIL_SLOT * dy : TAIL_SLOT * dy + chans - main, :] = w1[dy, dx, main:chans, :]

    tile = rows - 16

    def weight1(dx):
        return jnp.concatenate([w1[dy, dx, :main, :] for dy in range(3)] + [wt[dx]], axis=0)

    def weight2(dx):
        return jnp.concatenate([w2[dy, dx] for dy in range(3)], axis=0)

    def dot(lhs, rhs):
        return jnp.dot(lhs, rhs, preferred_element_type=F32)

    def pair_of(buffer, weight, ca, cb):
        acc = None
        for dx in range(3):
            lhs = jnp.concatenate([buffer[ca + dx], buffer[cb + dx]], axis=0)
            term = dot(lhs, weight(dx))
            acc = term if acc is None else acc + term
        return acc

    def edges_of(buffer, weight):
        both = jnp.concatenate([buffer[1], buffer[width]], axis=0)
        acc = dot(both, weight(1))
        part[0] = acc[:rows] + dot(buffer[2], weight(2))
        part[1] = acc[rows:] + dot(buffer[width - 1], weight(0))

    def activate(c, value):
        value = (gelu(value) * mcol[c]).astype(BF16)
        cols2[c + 1, :, hid : 2 * hid] = value
        value = value.astype(F32)
        build2(c + 1, value)

    def first(ca, cb):
        acc = pair_of(cols1, weight1, ca, cb) + b1_ref[...]
        pre[pl.ds(ca, 1), :] = acc[rows - 1 : rows, :]
        pre[pl.ds(cb, 1), :] = acc[2 * rows - 1 :, :]
        activate(ca, acc[:rows])
        activate(cb, acc[rows:])

    def edge(buffer, weight, side):
        slot, dx = ((0, 0), (width + 1, 2))[side]
        return part[side] + dot(buffer[slot], weight(dx))

    mask_top = mask[:, rows - 1 :]

    def first_edge(side):
        c = side * (width - 1)
        acc = edge(cols1, weight1, side) + b1_ref[...]
        pre[c : c + 1, :] = acc[rows - 1 :, :]
        activate(c, acc)

    def first_top():
        fold = [g * signs for g in ghosts(all1)]
        extra = pre[...]
        for dx in range(3):
            extra = extra + dot(twice(fold[dx][:, :main]), w1[2, dx, :main, :])[:width]
            extra = extra + dot(twice(fold[dx][:, main:]), wt[dx, LANES:, :])[:width]
        hidden = (gelu(extra) * mask_top).astype(BF16).astype(F32)
        top2[me] = hidden.astype(BF16)
        for c in range(width):
            old = cols2[c + 1, tile:, hid : 2 * hid].astype(F32)
            value = jnp.where(last_tile, hidden[c : c + 1], old)
            cols2[c + 1, tile:, hid : 2 * hid] = value.astype(BF16)
            down = jnp.where(last_tile, 0.0, pltpu.roll(value, 15, 0))
            cols2[c + 1, tile:, 2 * hid : 3 * hid] = down.astype(BF16)

    def put(c, value):
        for h in range(hid // LANES):
            part = value[:, h * LANES : (h + 1) * LANES]
            xs[h, pl.ds(c, rows, stride=width), :] = part

    def second(ca, cb):
        acc = pair_of(cols2, weight2, ca, cb) + b2_ref[...]
        put(ca, acc[:rows] * mcol[ca])
        put(cb, acc[rows:] * mcol[cb])

    def second_edge(side):
        c = side * (width - 1)
        put(c, (edge(cols2, weight2, side) + b2_ref[...]) * mcol[c])

    def second_top():
        fold = ghosts(all2)
        extra = None
        for dx in range(3):
            term = dot(twice(fold[dx]), w2[2, dx])[:width]
            extra = term if extra is None else extra + term
        extra = extra * mask_top
        for h in range(hid // LANES):
            at = (rows - 1) * width
            xs[h, at : at + width, :] += extra[:, h * LANES : (h + 1) * LANES]

    def inner(step, lo, hi):
        def one(i, _):
            step(2 * i + 1, 2 * i + 2)
            return 0

        lax.fori_loop(lo, hi, one, 0)

    pairs = (width - 2) // 2
    pl.semaphore_wait(barrier, n - 1)
    send_tops(top1, t1_send, t1_recv)
    for copy in x_halos:
        copy.start()
    edges_of(cols1, weight1)
    inner(first, 0, pairs)
    wait_tops(top1, t1_send, t1_recv)
    all1[...] = top1[...].astype(F32).reshape(all1.shape)
    for copy in x_halos:
        copy.wait()
    for side, slot in enumerate((0, width + 1)):
        mid = jnp.concatenate([cols1[slot, :, main : 2 * main], tails[slot]], axis=1)
        build1(slot, mid.astype(F32))
        first_edge(side)
    first_top()

    h_halos = [
        halo(cols2.at[1, :, mid2], cols2.at[width + 1, :, mid2], h_send, h_recv, 0, left),
        halo(cols2.at[width, :, mid2], cols2.at[0, :, mid2], h_send, h_recv, 1, right),
    ]
    send_tops(top2, t2_send, t2_recv)
    for copy in h_halos:
        copy.start()
    load_2.wait()
    edges_of(cols2, weight2)
    inner(second, 0, pairs)
    wait_tops(top2, t2_send, t2_recv)
    all2[...] = top2[...].astype(F32).reshape(all2.shape)
    for copy in h_halos:
        copy.wait()
    for side, slot in enumerate((0, width + 1)):
        build2(slot, cols2[slot, :, hid : 2 * hid].astype(F32))
        second_edge(side)
    second_top()
    for h in range(hid // LANES):
        block = xs[h, 0 : rows * width, :].reshape(rows, width, LANES)
        out_ref[:, :, h * LANES : (h + 1) * LANES] = block.astype(BF16)


def move(parts, src, dst, held, sems_in, sems_out):
    step = src.shape[0] // parts
    loads, stores = [], []
    for i in range(parts):
        at = pl.ds(i * step, step)
        loads.append(pltpu.make_async_copy(src.at[at], held.at[at], sems_in.at[i]))
        stores.append(pltpu.make_async_copy(held.at[at], dst.at[at], sems_out.at[i]))
        loads[-1].start()
    for load, store in zip(loads, stores):
        load.wait()
        store.start()
    for store in stores:
        store.wait()


def handed_on(array, parts):
    return pl.pallas_call(
        functools.partial(move, parts),
        out_shape=jax.ShapeDtypeStruct(array.shape, array.dtype),
        in_specs=[pl.BlockSpec(memory_space=pl.ANY)],
        out_specs=pl.BlockSpec(memory_space=pl.ANY),
        scratch_shapes=[
            pltpu.VMEM(array.shape, array.dtype),
            pltpu.SemaphoreType.DMA((parts,)),
            pltpu.SemaphoreType.DMA((parts,)),
        ],
        name="hand_on",
    )(array)


def local(n, state, ocean_mask, fold_map, w_first, b_first, w_second, b_second):
    rows, width, chans = state.shape
    hid = w_first.shape[-1]
    out = w_second.shape[-1]
    main = chans // LANES * LANES
    vmem = pl.BlockSpec(memory_space=pltpu.VMEM)
    hbm = pl.BlockSpec(memory_space=pl.ANY)
    result = pl.pallas_call(
        kernel,
        out_shape=jax.ShapeDtypeStruct((rows, width, out), BF16),
        in_specs=[hbm, vmem, pl.BlockSpec(memory_space=pltpu.SMEM), hbm, vmem, hbm, vmem],
        out_specs=vmem,
        scratch_shapes=[
            pltpu.VMEM((chans, width, rows), BF16),
            pltpu.VMEM((rows // LANES, (main + LANES) * width, LANES), F32),
            pltpu.VMEM(w_first.shape, BF16),
            pltpu.VMEM(w_second.shape, BF16),
            pltpu.VMEM((3, 2 * LANES, hid), BF16),
            pltpu.VMEM((width + 2, rows, 3 * main + 2 * LANES), BF16),
            pltpu.VMEM((width + 2, rows, LANES), BF16),
            pltpu.VMEM((width + 2, rows, 3 * hid), BF16),
            pltpu.VMEM((n, width, main + LANES), BF16),
            pltpu.VMEM((n, width, hid), BF16),
            pltpu.VMEM((width, main + LANES), F32),
            pltpu.VMEM((n * width, main + LANES), F32),
            pltpu.VMEM((n * width, hid), F32),
            pltpu.VMEM((2, rows, hid), F32),
            pltpu.VMEM((width, hid), F32),
            pltpu.VMEM((width, rows, 1), F32),
            pltpu.SemaphoreType.DMA((3,)),
            pltpu.SemaphoreType.DMA((n,)),
            pltpu.SemaphoreType.DMA((n,)),
            pltpu.SemaphoreType.DMA((n,)),
            pltpu.SemaphoreType.DMA((n,)),
            pltpu.SemaphoreType.DMA((4,)),
            pltpu.SemaphoreType.DMA((4,)),
            pltpu.SemaphoreType.DMA((2,)),
            pltpu.SemaphoreType.DMA((2,)),
        ],
        compiler_params=pltpu.CompilerParams(
            collective_id=0, has_side_effects=True, vmem_limit_bytes=56 * 1024 * 1024
        ),
        name="masked_conv_pair",
    )(
        jnp.transpose(state, (2, 1, 0)),
        jnp.transpose(ocean_mask),
        fold_map,
        w_first,
        b_first.reshape(1, hid),
        w_second,
        b_second.reshape(1, out),
    )
    return handed_on(result, 4)


def solution(mesh):
    return jax.shard_map(
        functools.partial(local, mesh.shape["lon"]),
        mesh=mesh,
        in_specs=(P(None, ("grp", "lon"), None), P(None, "lon"), P(), P(), P(), P(), P()),
        out_specs=P(None, ("grp", "lon"), None),
        check_vma=False,
    )
```
